32 devices in a mesh: parts: 2 (over y), dp: 4 (over x, core), tensor: 4 (over z).
Axes of the slice: x: 2, y: 2, z: 4, core: 2. Of those that a mesh axis runs over, the one named last changes fastest.
Arguments:
- layer_input: bfloat16 [16384, 8192], P(('parts', 'dp'), 'tensor'), parts along dimension 0, may hold values from -6 to 6
- up_grad: bfloat16 [16384, 28672], P(('parts', 'dp'), 'tensor'), parts along dimension 0, may hold values from -6 to 6
- hidden_input: bfloat16 [16384, 28672], P(('parts', 'dp'), 'tensor'), parts along dimension 0, may hold values from -6 to 6
- down_grad: bfloat16 [16384, 8192], P(('parts', 'dp'), 'tensor'), parts along dimension 0, may hold values from -6 to 6
- in_up: bfloat16 [128, 8192], P(None, 'tensor'), may hold values from -0.0625 to 0.0625
- out_up: bfloat16 [128, 28672], P(None, 'tensor'), may hold values from -0.03125 to 0.03125
- in_down: bfloat16 [128, 28672], P(None, 'tensor'), may hold values from -0.03125 to 0.03125
- out_down: bfloat16 [128, 8192], P(None, 'tensor'), may hold values from -0.0625 to 0.0625
- query_sketch: float32 [512, 2, 128, 128], P(('parts', 'dp'), None, 'tensor'), parts along dimension 0, may hold values from -6 to 6
Outputs:
- scores: float32 [64, 256], P(('parts', 'dp')), parts along dimension 0
The draws below stay inside these ranges and needn't reach their ends.
There are 2 independent parts, one for each index of `parts`. The reference program is written for one: setup_inputs(seed, part) draws one part's arguments, and reference() takes and returns one part's arrays. A program takes and returns all parts, laid end to end along the dimension named above; an argument that names none is the same for every part. Nothing has to cross between parts.
All inputs are finite; a program needn't handle non-finite values.
Results may differ from the reference program's by a relative error of at most 0.0003.
Values sent between devices are 32-bit elements; how exact they have to be, the bound alone decides.
No kernel may reach another device: no remote copies, remote signals or barrier semaphores. Data moves between devices by JAX's collectives and lax.ppermute only.
A program may use at most 192 MiB of HBM per device.

```python
import jax
import jax.numpy as jnp
from jax import lax

D = 8192
FF = 28672
K = 128
LEN = 256
EXAMPLES = 32
QUERIES = 256
TOKENS = 8192


def block_levels(key, dims, split, smallest, top_value):
    factor_of = 1.0
    for position, blocks in split:
        draws = jax.random.uniform(jax.random.fold_in(jax.random.fold_in(key, 6), position), (blocks,), jnp.float32, smallest / len(split), top_value / len(split))
        factor_of = factor_of * jnp.repeat(jnp.exp(draws), dims[position] // blocks).reshape((-1,) + (1,) * (len(dims) - 1 - position))
    return factor_of


def centred(key, shape, scale, bound, shards=(), dtype=jnp.bfloat16):
    drawn = scale * jax.random.normal(key, shape, jnp.float32)
    if shards:
        drawn = drawn * block_levels(key, shape, shards, -0.22, 0.18)
    return jnp.clip(drawn, -bound, bound).astype(dtype)


def setup_inputs(seed: int = 0, part: int = 0) -> dict:
    splits = jax.random.split(jax.random.key(seed), 10)
    part_splits = jax.random.split(jax.random.fold_in(splits[9], part), 10)
    return {
        "layer_input": centred(part_splits[0], (TOKENS, D), 1.0, 6.0, ((0, 4), (1, 4))),
        "up_grad": centred(part_splits[1], (TOKENS, FF), 1.0, 6.0, ((0, 4), (1, 4))),
        "hidden_input": centred(part_splits[2], (TOKENS, FF), 1.0, 6.0, ((0, 4), (1, 4))),
        "down_grad": centred(part_splits[3], (TOKENS, D), 1.0, 6.0, ((0, 4), (1, 4))),
        "in_up": centred(splits[4], (K, D), D ** -0.5, 0.0625, ((1, 4),)),
        "out_up": centred(splits[5], (K, FF), FF ** -0.5, 0.03125, ((1, 4),)),
        "in_down": centred(splits[6], (K, FF), FF ** -0.5, 0.03125, ((1, 4),)),
        "out_down": centred(splits[7], (K, D), D ** -0.5, 0.0625, ((1, 4),)),
        "query_sketch": centred(part_splits[8], (QUERIES, 2, K, K), 1.0, 6.0, ((0, 4), (2, 4)), jnp.float32),
    }


def project(act, proj):
    return jnp.dot(act, proj.T, preferred_element_type=jnp.float32)

def layer_sketch(left, right):
    left3 = left.reshape(EXAMPLES, LEN, K)
    right3 = right.reshape(EXAMPLES, LEN, K)
    return jnp.einsum('elr,elc->erc', left3, right3, precision=lax.Precision.HIGHEST) / jnp.sqrt(jnp.float32(LEN))

def reference(layer_input, up_grad, hidden_input, down_grad, in_up, out_up, in_down, out_down, query_sketch):
    a_up = project(layer_input, in_up)
    b_up = project(up_grad, out_up)
    a_down = project(hidden_input, in_down)
    b_down = project(down_grad, out_down)
    sketch = jnp.stack([layer_sketch(a_up, b_up), layer_sketch(a_down, b_down)], axis=1)
    total = jnp.einsum('elrc,qlrc->eq', sketch, query_sketch, precision=lax.Precision.HIGHEST)
    return total / jnp.float32(K)
```

```python
import functools

import jax
import jax.numpy as jnp
from jax import lax
from jax.experimental import pallas as pl
from jax.experimental.pallas import tpu as pltpu
from jax.sharding import PartitionSpec as P

K = 128
LEN = 256
LAG = 3
PIECE = 1024
AHEAD = 4
ROWS_BY_ROWS = (((1,), (1,)), ((), ()))
SIDES = [(0, 1), (1, 0), (2, 3), (3, 2)]
MIDDLE = [(1, 2), (2, 1)]
SKIP = [(0, 2), (3, 1)]
ENDS = [(0, 3), (3, 0)]

WHOLE = pl.BlockSpec(memory_space=pltpu.VMEM)
SCALARS = pl.BlockSpec(memory_space=pltpu.SMEM)
ANYWHERE = pl.BlockSpec(memory_space=pl.ANY)


def send(x, pairs):
    return lax.ppermute(x, "tensor", pairs)


def halves(x):
    high = x.astype(jnp.bfloat16)
    return high, (x - high.astype(jnp.float32)).astype(jnp.bfloat16)


def pieces(width):
    return [(lo, min(lo + PIECE, width)) for lo in range(0, width, PIECE)]


def project_kernel(blocks, index, left, right, p_left, p_right, *refs):
    outs, (held_left, held_right, sem) = refs[:blocks], refs[blocks:]
    steps = []
    for x, held, p, row in ((left, held_left, p_left, 0), (right, held_right, p_right, K)):
        for lo, hi in pieces(x.shape[1]):
            copies = [
                pltpu.make_async_copy(
                    x.at[pl.ds(pl.multiple_of(index[i] * LEN, LEN), LEN), lo:hi],
                    held.at[i * LEN : (i + 1) * LEN, lo:hi],
                    sem.at[len(steps) * blocks + i],
                )
                for i in range(blocks)
            ]
            steps.append((copies, held, p, row, lo, hi))
    for step in steps[:AHEAD]:
        for copy in step[0]:
            copy.start()
    for n, (copies, held, p, row, lo, hi) in enumerate(steps):
        for copy in copies:
            copy.wait()
        if n + AHEAD < len(steps):
            for copy in steps[n + AHEAD][0]:
                copy.start()
        part = lax.dot_general(
            p[:, lo:hi], held[:, lo:hi], ROWS_BY_ROWS, preferred_element_type=jnp.float32
        )
        for i, out in enumerate(outs):
            if lo == 0:
                out[row : row + K, :] = part[:, i * LEN : (i + 1) * LEN]
            else:
                out[row : row + K, :] += part[:, i * LEN : (i + 1) * LEN]


def project(index, left, right, p_left, p_right):
    blocks = index.shape[0]
    widths = left.shape[1], right.shape[1]
    rows = blocks * LEN
    copies = blocks * sum(len(pieces(w)) for w in widths)
    return pl.pallas_call(
        functools.partial(project_kernel, blocks),
        in_specs=[SCALARS, ANYWHERE, ANYWHERE, WHOLE, WHOLE],
        out_specs=[WHOLE] * blocks,
        out_shape=[pltpu.VMEM((2 * K, LEN), jnp.float32)] * blocks,
        scratch_shapes=[
            pltpu.VMEM((rows, widths[0]), left.dtype),
            pltpu.VMEM((rows, widths[1]), right.dtype),
            pltpu.SemaphoreType.DMA((copies,)),
        ],
        compiler_params=pltpu.CompilerParams(vmem_limit_bytes=44 * 2**20),
        cost_estimate=pl.CostEstimate(
            flops=2 * rows * K * sum(widths), bytes_accessed=2 * rows * sum(widths), transcendentals=0
        ),
    )(index, left, right, p_left, p_right)


def sketch_kernel(count, width, dest, *refs):
    own, got, outs, full = refs[:count], refs[count : 2 * count], refs[2 * count : -1], refs[-1]
    for i in range(count):
        both = own[i][...] + got[i][...]
        high, low = halves(both)
        a = jnp.concatenate([high[:K], low[:K]], 0)
        b = jnp.concatenate([high[K:], low[K:]], 0)
        s = lax.dot_general(a, b, ROWS_BY_ROWS, preferred_element_type=jnp.float32)
        full[...] = s[:K, :K] + (s[:K, K:] + s[K:, :K] + s[K:, K:])
        for n, out in enumerate(outs):
            out[i] = full[pl.ds(pl.multiple_of(dest[n] * width, 8), width), :]


def sketches(dest, own, got, width):
    count = len(own)
    return pl.pallas_call(
        functools.partial(sketch_kernel, count, width),
        in_specs=[SCALARS] + [WHOLE] * (2 * count),
        out_specs=[WHOLE] * 4,
        out_shape=[pltpu.VMEM((count, width, K), jnp.float32)] * 4,
        scratch_shapes=[pltpu.VMEM((K, K), jnp.float32)],
        cost_estimate=pl.CostEstimate(
            flops=8 * count * LEN * K * K, bytes_accessed=count * 2**19, transcendentals=0
        ),
    )(dest, *own, *got)


def score_kernel(steps, rows, place, *refs):
    (cuts, queries, out, cat, total) = refs[:-4], *refs[-4:]
    k = pl.program_id(0)
    half = cuts[0].shape[0]

    def gather(layer, first):
        own, near, skip, across = cuts[4 * layer : 4 * layer + 4]
        for i in range(rows):
            r = first + i
            lanes = slice(i * K, (i + 1) * K)
            home = jnp.where(place[0] == 1, own[:, r, :], near[:, r, :])
            far = jnp.where(place[0] == 1, across[:, r, :], skip[:, r, :])
            high, low = halves(jnp.concatenate([home, far], 0))
            cat[: 2 * half, lanes] = high.astype(jnp.float32)
            cat[2 * half :, lanes] = low.astype(jnp.float32)

    for step in range(steps):

        @pl.when(k == step)
        def _():
            layer, part = divmod(step, steps // 2)
            gather(layer, part * rows)

    s = cat[...].astype(jnp.bfloat16)
    high, low = halves(queries[...])
    d = lax.dot_general(s, high, ROWS_BY_ROWS, preferred_element_type=jnp.float32)
    d += lax.dot_general(s, low, ROWS_BY_ROWS, preferred_element_type=jnp.float32)
    d = d[: 2 * half] + d[2 * half :]

    @pl.when(k == 0)
    def _():
        total[...] = d

    @pl.when(k > 0)
    def _():
        total[...] += d

    @pl.when(k == steps - 1)
    def _():
        t = total[...] * (1.0 / (LEN**0.5 * K))
        swapped = jnp.concatenate([t[half:], t[:half]], 0)
        out[...] = jnp.where(place[1] == 1, t, swapped)


def score(place, cuts, queries):
    half, width, _ = cuts[0].shape
    count, depth = queries.shape
    steps = 4
    rows = 2 * width // steps
    return pl.pallas_call(
        functools.partial(score_kernel, steps, rows),
        grid=(steps,),
        in_specs=[SCALARS]
        + [WHOLE] * len(cuts)
        + [pl.BlockSpec((count, depth // steps), lambda k: (0, k))],
        out_specs=WHOLE,
        out_shape=jax.ShapeDtypeStruct((2 * half, count), jnp.float32),
        scratch_shapes=[
            pltpu.VMEM((4 * half, depth // steps), jnp.float32),
            pltpu.VMEM((2 * half, count), jnp.float32),
        ],
        cost_estimate=pl.CostEstimate(
            flops=64 * count * depth, bytes_accessed=4 * count * depth, transcendentals=0
        ),
    )(place, *cuts, queries)


def line(
    layer_input, up_grad, hidden_input, down_grad, in_up, out_up, in_down, out_down, query_sketch
):
    half = layer_input.shape[0] // LEN // 2
    width = K // lax.axis_size("tensor")
    z = lax.axis_index("tensor")
    on_left = z < 2
    at_end = (z == 0) | (z == 3)
    far = jnp.where(on_left, half, 0).astype(jnp.int32)
    home = half - far
    local_queries = query_sketch.shape[0]
    queries = lax.all_gather(query_sketch.reshape(local_queries, -1), "dp", axis=0, tiled=True)

    keep = lambda x: pltpu.with_memory_space_constraint(x, pltpu.VMEM)
    layers = (
        (layer_input, up_grad, keep(in_up), keep(out_up)),
        (hidden_input, down_grad, keep(in_down), keep(out_down)),
    )
    forward, backward = [], []
    for layer, group in ((0, [0]), (0, [1]), (0, [2, 3]), (1, [0, 1]), (1, [2, 3])):
        index = jnp.stack([far + e for e in group] + [home + e for e in group])
        outs = project(index, *layers[layer])
        forward += outs[: len(group)]
        backward += outs[len(group) :]

    chunks = len(forward)
    side, middle = {}, {}
    for k in range(chunks + LAG):
        done = k - LAG
        load = forward[k] if k < chunks else None
        if done >= 0:
            back = backward[done] + middle[done]
            load = back if load is None else jnp.where(at_end, load, back)
        side[k] = send(load, SIDES)
        if 1 <= k <= chunks:
            middle[k - 1] = send(forward[k - 1] + side[k - 1], MIDDLE)

    dest = jnp.stack([z, z ^ 1, z ^ 2, 3 - z]).astype(jnp.int32)
    cuts = []
    for layer in range(2):
        mine = range(layer * half, (layer + 1) * half)
        own, near, skip, across = sketches(
            dest, [backward[i] for i in mine], [side[i + LAG] for i in mine], width
        )
        cuts += [own, send(near, SIDES), send(skip, SKIP), send(across, ENDS)]
    place = jnp.stack([at_end, on_left]).astype(jnp.int32)
    return lax.psum(score(place, cuts, queries), "tensor")


def own_rows(full, width):
    return lax.dynamic_slice_in_dim(full, lax.axis_index("tensor") * width, width, 1)


def layer_sketch(left, right, examples):
    left3 = left.reshape(examples, LEN, left.shape[1])
    right3 = right.reshape(examples, LEN, right.shape[1])
    return jnp.einsum("elr,elc->erc", left3, right3, precision=lax.Precision.HIGHEST) / jnp.sqrt(
        jnp.float32(LEN)
    )


def wide(
    layer_input, up_grad, hidden_input, down_grad, in_up, out_up, in_down, out_down, query_sketch
):
    width = K // lax.axis_size("tensor")
    examples = layer_input.shape[0] // LEN
    pairs = (
        (layer_input, in_up),
        (up_grad, out_up),
        (hidden_input, in_down),
        (down_grad, out_down),
    )
    a_up, b_up, a_down, b_down = lax.psum(
        tuple(jnp.dot(x, p.T, preferred_element_type=jnp.float32) for x, p in pairs), "tensor"
    )
    sketch = jnp.stack(
        [
            layer_sketch(own_rows(a_up, width), b_up, examples),
            layer_sketch(own_rows(a_down, width), b_down, examples),
        ],
        axis=1,
    )
    partial_total = jnp.einsum(
        "elrc,qlrc->qe",
        sketch,
        lax.all_gather(query_sketch, "dp", axis=0, tiled=True),
        precision=lax.Precision.HIGHEST,
    )
    return lax.psum(partial_total, "tensor").T / jnp.float32(K)


def solution(mesh):
    placed = (
        P(("parts", "dp"), "tensor"),
        P(("parts", "dp"), "tensor"),
        P(("parts", "dp"), "tensor"),
        P(("parts", "dp"), "tensor"),
        P(None, "tensor"),
        P(None, "tensor"),
        P(None, "tensor"),
        P(None, "tensor"),
        P(("parts", "dp"), None, "tensor", None),
    )
    return jax.shard_map(
        line if mesh.shape["tensor"] == 4 else wide,
        mesh=mesh,
        in_specs=placed,
        out_specs=P(("parts", "dp"), None),
        check_vma=False,
    )
```

```python
import functools

import jax
import jax.numpy as jnp
from jax import lax
from jax.experimental import pallas as pl
from jax.experimental.pallas import tpu as pltpu
from jax.sharding import PartitionSpec as P

K = 128
LEN = 256
PIECE = 1024
AHEAD = 4
ROWS_BY_ROWS = (((1,), (1,)), ((), ()))
NEAR = [(0, 1), (1, 0), (2, 3), (3, 2)]
SKIP = [(0, 2), (2, 0), (1, 3), (3, 1)]
ACROSS = [(0, 3), (3, 0), (1, 2), (2, 1)]

WHOLE = pl.BlockSpec(memory_space=pltpu.VMEM)
SCALARS = pl.BlockSpec(memory_space=pltpu.SMEM)
OUTSIDE = pl.BlockSpec(memory_space=pltpu.HBM)


def here(x):
    return pltpu.with_memory_space_constraint(x, pltpu.VMEM)


def there(x):
    return pltpu.with_memory_space_constraint(x, pltpu.HBM)


def send(x, pairs, axis="tensor"):
    return lax.ppermute(x, axis, pairs)


def halves(x):
    high = x.astype(jnp.bfloat16)
    return high, (x - high.astype(jnp.float32)).astype(jnp.bfloat16)


def pieces(width):
    return [(lo, min(lo + PIECE, width)) for lo in range(0, width, PIECE)]


def project_kernel(shapes, load, spread, index, left, right, p_left, p_right, *refs):
    moves = []
    if spread:
        queries, refs = refs[0], refs[1:]
        flat, spread_sem = refs[len(shapes)], refs[-1]
        refs = refs[: len(shapes)] + refs[len(shapes) + 1 : -1]
        for r in range(queries.shape[1]):
            moves.append(
                pltpu.make_async_copy(
                    queries.at[:, r, :], flat.at[:, r * K : (r + 1) * K], spread_sem.at[r]
                )
            )
    arrays, (slots, sem, *loaded) = refs[: len(shapes)], refs[len(shapes) :]
    outs = [array.at[i] for array, n in zip(arrays, shapes) for i in range(n)]
    depth = slots.shape[0]
    steps = []
    for first in range(0, len(outs), 2):
        group = range(first, min(first + 2, len(outs)))
        for side, (x, p, row) in enumerate(((left, p_left, 0), (right, p_right, K))):
            for lo, hi in pieces(x.shape[1]):
                slot = len(steps) % depth
                copies = [
                    pltpu.make_async_copy(
                        x.at[pl.ds(pl.multiple_of(index[i] * LEN, LEN), LEN), lo:hi],
                        slots.at[slot, n * LEN : (n + 1) * LEN, : hi - lo],
                        sem.at[slot, n],
                    )
                    for n, i in enumerate(group)
                ]
                if load and first == 0:
                    copies.append(
                        pltpu.make_async_copy(
                            p.at[:, lo:hi], loaded[side].at[:, lo:hi], sem.at[slot, 2]
                        )
                    )
                steps.append((copies, slot, group, loaded[side] if load else p, row, lo, hi))
    for step in steps[: depth - 1]:
        for copy in step[0]:
            copy.start()
    for move in moves:
        move.start()
    for n, (copies, slot, group, p, row, lo, hi) in enumerate(steps):
        for copy in copies:
            copy.wait()
        if n + depth - 1 < len(steps):
            for copy in steps[n + depth - 1][0]:
                copy.start()
        part = lax.dot_general(
            p[:, lo:hi],
            slots[slot, : len(group) * LEN, : hi - lo],
            ROWS_BY_ROWS,
            preferred_element_type=jnp.float32,
        )
        for m, i in enumerate(group):
            if lo == 0:
                outs[i][row : row + K, :] = part[:, m * LEN : (m + 1) * LEN]
            else:
                outs[i][row : row + K, :] += part[:, m * LEN : (m + 1) * LEN]
    for move in moves:
        move.wait()


def project(groups, left, right, p_left, p_right, load=False, after=None, queries=None):
    shapes = [len(group) for group in groups]
    index = jnp.stack([i for group in groups for i in group]).astype(jnp.int32)
    if after is not None:
        index = lax.optimization_barrier((index, after))[0]
    widths = left.shape[1], right.shape[1]
    rows = sum(shapes) * LEN
    place = there if load else here
    scratch = [
        pltpu.VMEM((AHEAD + 1, 2 * LEN, PIECE), left.dtype),
        pltpu.SemaphoreType.DMA((AHEAD + 1, 3)),
    ]
    if load:
        scratch += [pltpu.VMEM((K, w), left.dtype) for w in widths]
    p_spec = OUTSIDE if load else WHOLE
    more_in, more_out = [], []
    if queries is not None:
        more_in = [there(queries)]
        count, per_query, _ = queries.shape
        more_out = [pltpu.VMEM((count, per_query * K), queries.dtype)]
        scratch += [pltpu.SemaphoreType.DMA((per_query,))]
    return pl.pallas_call(
        functools.partial(project_kernel, shapes, load, queries is not None),
        in_specs=[SCALARS, OUTSIDE, OUTSIDE, p_spec, p_spec] + [OUTSIDE] * len(more_in),
        out_specs=[WHOLE] * (len(shapes) + len(more_out)),
        out_shape=[pltpu.VMEM((n, 2 * K, LEN), jnp.float32) for n in shapes] + more_out,
        scratch_shapes=scratch,
        compiler_params=pltpu.CompilerParams(vmem_limit_bytes=16 * 2**20),
        cost_estimate=pl.CostEstimate(
            flops=2 * rows * K * sum(widths), bytes_accessed=2 * rows * sum(widths), transcendentals=0
        ),
    )(index, there(left), there(right), place(p_left), place(p_right), *more_in)


def sketch_kernel(count, width, dest, *refs):
    own, first, second, outs, full = (
        refs[:count],
        refs[count : 2 * count],
        refs[2 * count : 3 * count],
        refs[3 * count : -1],
        refs[-1],
    )
    for i in range(count):
        high, low = halves(own[i][0] + first[i][0] + second[i][...])
        a = jnp.concatenate([high[:K], low[:K]], 0)
        b = jnp.concatenate([high[K:], low[K:]], 0)
        s = lax.dot_general(a, b, ROWS_BY_ROWS, preferred_element_type=jnp.float32)
        full[...] = s[:K, :K] + (s[:K, K:] + s[K:, :K] + s[K:, K:])
        for n, out in enumerate(outs):
            out[i] = full[pl.ds(pl.multiple_of(dest[n] * width, 8), width), :]


def sketches(dest, own, first, second, width):
    count = len(own)
    return pl.pallas_call(
        functools.partial(sketch_kernel, count, width),
        in_specs=[SCALARS] + [WHOLE] * (3 * count),
        out_specs=[WHOLE] * 4,
        out_shape=[pltpu.VMEM((count, width, K), jnp.float32)] * 4,
        scratch_shapes=[pltpu.VMEM((K, K), jnp.float32)],
        cost_estimate=pl.CostEstimate(
            flops=8 * count * LEN * K * K, bytes_accessed=count * 2**19, transcendentals=0
        ),
    )(dest, *own, *first, *second)


def split_kernel(place, mine, other, high, low):
    count, depth = mine.shape
    for n, x in enumerate((mine, other)):
        at = pl.ds(pl.multiple_of((place[0] ^ n) * count, 16), count)
        for lo in range(0, depth, 512):
            h, l = halves(x[:, lo : lo + 512])
            high[at, lo : lo + 512] = h
            low[at, lo : lo + 512] = l


def split(core, mine, other, after=None):
    count, depth = mine.shape
    if after is not None:
        core = lax.optimization_barrier((core, after))[0]
    return pl.pallas_call(
        split_kernel,
        in_specs=[SCALARS, WHOLE, WHOLE],
        out_specs=[WHOLE] * 2,
        out_shape=[pltpu.VMEM((2 * count, depth), jnp.bfloat16)] * 2,
        compiler_params=pltpu.CompilerParams(vmem_limit_bytes=16 * 2**20),
        cost_estimate=pl.CostEstimate(
            flops=8 * count * depth, bytes_accessed=16 * count * depth, transcendentals=0
        ),
    )(core, mine, other)


def score_kernel(pair, place, own, near, skip, across, *refs):
    parts, out, cat = refs[:4], refs[4], refs[5]
    z, chip = place[0], place[1]
    width = own.shape[1]
    count = 4 * pair
    for layer in range(2):
        for r in range(width):
            lanes = slice((layer * width + r) * K, (layer * width + r + 1) * K)
            mine = slice(layer * pair, (layer + 1) * pair)
            cut = [x[mine, r, :] for x in (own, near, skip, across)]
            for b in range(4):
                pick = jnp.where(z == b ^ 2, cut[2], jnp.where(z == 3 - b, cut[3], cut[0]))
                high, low = halves(jnp.where(z == b ^ 1, cut[1], pick))
                cat[b * pair : (b + 1) * pair, lanes] = high.astype(jnp.float32)
                cat[count + b * pair : count + (b + 1) * pair, lanes] = low.astype(jnp.float32)
    s = cat[...].astype(jnp.bfloat16)
    totals = []
    for high, low in (parts[:2], parts[2:]):
        d = lax.dot_general(s, high[...], ROWS_BY_ROWS, preferred_element_type=jnp.float32)
        d += lax.dot_general(s, low[...], ROWS_BY_ROWS, preferred_element_type=jnp.float32)
        totals.append((d[:count] + d[count:]) * (1.0 / (LEN**0.5 * K)))
    mine, other = totals
    out[...] = jnp.concatenate(
        [jnp.where(chip == 0, mine, other), jnp.where(chip == 0, other, mine)], 1
    )


def score(place, cuts, parts, pair):
    queries, depth = parts[0].shape
    return pl.pallas_call(
        functools.partial(score_kernel, pair),
        in_specs=[SCALARS] + [WHOLE] * 8,
        out_specs=WHOLE,
        out_shape=pltpu.VMEM((4 * pair, 2 * queries), jnp.float32),
        scratch_shapes=[pltpu.VMEM((8 * pair, depth), jnp.float32)],
        compiler_params=pltpu.CompilerParams(vmem_limit_bytes=24 * 2**20),
        cost_estimate=pl.CostEstimate(
            flops=64 * queries * depth, bytes_accessed=8 * queries * depth, transcendentals=0
        ),
    )(place, *cuts, *parts)


def line(
    layer_input, up_grad, hidden_input, down_grad, in_up, out_up, in_down, out_down, query_sketch
):
    pair = layer_input.shape[0] // LEN // 4
    width = K // 4
    z = lax.axis_index("tensor").astype(jnp.int32)
    dp = lax.axis_index("dp").astype(jnp.int32)
    up = (layer_input, up_grad, in_up, out_up)
    down = (hidden_input, down_grad, in_down, out_down)

    def of(owner, j):
        return owner * pair + j

    def leaving(j):
        return [of(z ^ 1, j), of(z ^ 2, j)]

    def staying(j):
        return [of(z, j), of(3 - z, j)]

    queries = query_sketch.reshape(query_sketch.shape[0], -1, K)
    by_core = [(0, 1), (1, 0), (2, 3), (3, 2)]
    by_chip = [(0, 2), (2, 0), (1, 3), (3, 1)]
    core = (dp & 1).reshape(1)

    def across(stay, first, after=None):
        if after is not None:
            stay = lax.optimization_barrier((stay, after))[0]
        return stay[1] + first[1]

    (out_0,) = project([leaving(0)], *up, load=True)
    first_0 = send(out_0, NEAR)
    out_1, flat = project([leaving(1)], *up, after=out_0, queries=queries)
    first_1 = send(out_1, NEAR)
    other_core = send(flat, by_core, "dp")
    other_chip = send(flat, by_chip, "dp")
    stay_0, stay_1 = project([staying(0), staying(1)], *up, after=(out_1, first_0))
    sum_0 = across(stay_0, first_0)
    second_0 = send(sum_0, ACROSS)
    sum_1 = across(stay_1, first_1)
    second_1 = send(sum_1, ACROSS)
    out_2, stay_2 = project([leaving(0), staying(0)], *down, after=(sum_0, sum_1))
    first_2 = send(out_2, NEAR)
    out_3, stay_3 = project([leaving(1), staying(1)], *down, after=(out_2, second_0))
    first_3 = send(out_3, NEAR)
    sum_2 = across(stay_2, first_2, (out_3, second_1))
    second_2 = send(sum_2, ACROSS)
    own_chip = split(core, flat, other_core, after=sum_2)
    sum_3 = across(stay_3, first_3, own_chip[0])
    second_3 = send(sum_3, ACROSS)
    other_chip = lax.optimization_barrier((other_chip, sum_3))[0]
    other_both = send(other_chip, by_core, "dp")
    parts = own_chip + split(core, other_chip, other_both, after=second_2)
    stay = [stay_0, stay_1, stay_2, stay_3]
    first = [first_0, first_1, first_2, first_3]
    second = [second_0, second_1, second_2, second_3]

    dest = jnp.stack([z, z ^ 1, z ^ 2, 3 - z])
    own, near, skip, far = sketches(dest, stay, first, second, width)
    cuts = [own, send(near, NEAR), send(skip, SKIP), send(far, ACROSS)]
    partial = score(jnp.stack([z, dp >> 1]), cuts, parts, pair)
    partial = partial + send(partial, NEAR)
    return partial + send(partial, SKIP)


def own_rows(full, width):
    return lax.dynamic_slice_in_dim(full, lax.axis_index("tensor") * width, width, 1)


def layer_sketch(left, right, examples):
    left3 = left.reshape(examples, LEN, left.shape[1])
    right3 = right.reshape(examples, LEN, right.shape[1])
    return jnp.einsum("elr,elc->erc", left3, right3, precision=lax.Precision.HIGHEST) / jnp.sqrt(
        jnp.float32(LEN)
    )


def wide(
    layer_input, up_grad, hidden_input, down_grad, in_up, out_up, in_down, out_down, query_sketch
):
    width = K // lax.axis_size("tensor")
    examples = layer_input.shape[0] // LEN
    pairs = (
        (layer_input, in_up),
        (up_grad, out_up),
        (hidden_input, in_down),
        (down_grad, out_down),
    )
    a_up, b_up, a_down, b_down = lax.psum(
        tuple(jnp.dot(x, p.T, preferred_element_type=jnp.float32) for x, p in pairs), "tensor"
    )
    sketch = jnp.stack(
        [
            layer_sketch(own_rows(a_up, width), b_up, examples),
            layer_sketch(own_rows(a_down, width), b_down, examples),
        ],
        axis=1,
    )
    partial_total = jnp.einsum(
        "elrc,qlrc->qe",
        sketch,
        lax.all_gather(query_sketch, "dp", axis=0, tiled=True),
        precision=lax.Precision.HIGHEST,
    )
    return lax.psum(partial_total, "tensor").T / jnp.float32(K)


def solution(mesh):
    placed = (
        P(("parts", "dp"), "tensor"),
        P(("parts", "dp"), "tensor"),
        P(("parts", "dp"), "tensor"),
        P(("parts", "dp"), "tensor"),
        P(None, "tensor"),
        P(None, "tensor"),
        P(None, "tensor"),
        P(None, "tensor"),
        P(("parts", "dp"), None, "tensor", None),
    )
    return jax.shard_map(
        line if mesh.shape["tensor"] == 4 and mesh.shape["dp"] == 4 else wide,
        mesh=mesh,
        in_specs=placed,
        out_specs=P(("parts", "dp"), None),
        check_vma=False,
    )
```

```python
import functools

import jax
import jax.numpy as jnp
from jax import lax
from jax.experimental import pallas as pl
from jax.experimental.pallas import tpu as pltpu
from jax.sharding import PartitionSpec as P

K = 128
LEN = 256
PIECE = 1024
AHEAD = 4
ROWS_BY_ROWS = (((1,), (1,)), ((), ()))
NEAR = [(0, 1), (1, 0), (2, 3), (3, 2)]
SKIP = [(0, 2), (2, 0), (1, 3), (3, 1)]
ACROSS = [(0, 3), (3, 0), (1, 2), (2, 1)]

WHOLE = pl.BlockSpec(memory_space=pltpu.VMEM)
SCALARS = pl.BlockSpec(memory_space=pltpu.SMEM)
OUTSIDE = pl.BlockSpec(memory_space=pltpu.HBM)


def here(x):
    return pltpu.with_memory_space_constraint(x, pltpu.VMEM)


def there(x):
    return pltpu.with_memory_space_constraint(x, pltpu.HBM)


def send(x, pairs, axis="tensor"):
    return lax.ppermute(x, axis, pairs)


def halves(x):
    high = x.astype(jnp.bfloat16)
    return high, (x - high.astype(jnp.float32)).astype(jnp.bfloat16)


def pieces(width):
    return [(lo, min(lo + PIECE, width)) for lo in range(0, width, PIECE)]


def project_kernel(jobs, load, spread, index, *refs):
    operands, refs = refs[:8], refs[8:]
    moves = []
    if spread:
        queries, refs = refs[0], refs[1:]
        flat, spread_sem = refs[len(jobs)], refs[-1]
        refs = refs[: len(jobs)] + refs[len(jobs) + 1 : -1]
        for r in range(queries.shape[1]):
            moves.append(
                pltpu.make_async_copy(
                    queries.at[:, r, :], flat.at[:, r * K : (r + 1) * K], spread_sem.at[r]
                )
            )
    arrays, (slots, sem, *loaded) = refs[: len(jobs)], refs[len(jobs) :]
    depth = slots.shape[0]
    steps = []
    number = 0
    for array, (layer, count) in zip(arrays, jobs):
        left, right, p_left, p_right = operands[4 * layer : 4 * layer + 4]
        for first in range(0, count, 2):
            group = range(first, min(first + 2, count))
            for side, (x, p, row) in enumerate(((left, p_left, 0), (right, p_right, K))):
                for lo, hi in pieces(x.shape[1]):
                    slot = len(steps) % depth
                    copies = [
                        pltpu.make_async_copy(
                            x.at[pl.ds(pl.multiple_of(index[number + i] * LEN, LEN), LEN), lo:hi],
                            slots.at[slot, n * LEN : (n + 1) * LEN, : hi - lo],
                            sem.at[slot, n],
                        )
                        for n, i in enumerate(group)
                    ]
                    if load and first == 0:
                        copies.append(
                            pltpu.make_async_copy(
                                p.at[:, lo:hi], loaded[side].at[:, lo:hi], sem.at[slot, 2]
                            )
                        )
                    outs = [array.at[i] for i in group]
                    steps.append((copies, slot, outs, loaded[side] if load else p, row, lo, hi))
        number += count
    for step in steps[: depth - 1]:
        for copy in step[0]:
            copy.start()
    for move in moves:
        move.start()
    for n, (copies, slot, outs, p, row, lo, hi) in enumerate(steps):
        for copy in copies:
            copy.wait()
        if n + depth - 1 < len(steps):
            for copy in steps[n + depth - 1][0]:
                copy.start()
        part = lax.dot_general(
            p[:, lo:hi],
            slots[slot, : len(outs) * LEN, : hi - lo],
            ROWS_BY_ROWS,
            preferred_element_type=jnp.float32,
        )
        for m, out in enumerate(outs):
            if lo == 0:
                out[row : row + K, :] = part[:, m * LEN : (m + 1) * LEN]
            else:
                out[row : row + K, :] += part[:, m * LEN : (m + 1) * LEN]
    for move in moves:
        move.wait()


def project(layers, jobs, load=False, after=None, queries=None):
    index = jnp.stack([i for _, group in jobs for i in group]).astype(jnp.int32)
    if after is not None:
        index = lax.optimization_barrier((index, after))[0]
    jobs = [(layer, len(group)) for layer, group in jobs]
    dtype = layers[0][0].dtype
    scratch = [
        pltpu.VMEM((AHEAD + 1, 2 * LEN, PIECE), dtype),
        pltpu.SemaphoreType.DMA((AHEAD + 1, 3)),
    ]
    if load:
        scratch += [pltpu.VMEM(p.shape, dtype) for p in layers[jobs[0][0]][2:]]
    place = there if load else here
    operands, specs = [], []
    for layer, (left, right, p_left, p_right) in enumerate(layers):
        used = layer in [job[0] for job in jobs]
        operands += [there(left), there(right)]
        operands += [place(p) if used else there(p) for p in (p_left, p_right)]
        specs += [OUTSIDE, OUTSIDE] + [OUTSIDE if load or not used else WHOLE] * 2
    extra = []
    if queries is not None:
        operands.append(there(queries))
        specs.append(OUTSIDE)
        count, per_query, _ = queries.shape
        extra = [pltpu.VMEM((count, per_query * K), queries.dtype)]
        scratch.append(pltpu.SemaphoreType.DMA((per_query,)))
    return pl.pallas_call(
        functools.partial(project_kernel, jobs, load, queries is not None),
        in_specs=[SCALARS] + specs,
        out_specs=[WHOLE] * (len(jobs) + len(extra)),
        out_shape=[pltpu.VMEM((n, 2 * K, LEN), jnp.float32) for _, n in jobs] + extra,
        scratch_shapes=scratch,
        compiler_params=pltpu.CompilerParams(vmem_limit_bytes=16 * 2**20),
        cost_estimate=pl.CostEstimate(
            flops=sum(
                2 * n * LEN * K * (layers[layer][0].shape[1] + layers[layer][1].shape[1])
                for layer, n in jobs
            ),
            bytes_accessed=sum(
                2 * n * LEN * (layers[layer][0].shape[1] + layers[layer][1].shape[1])
                for layer, n in jobs
            ),
            transcendentals=0,
        ),
    )(index, *operands)


def sketch_kernel(count, width, dest, *refs):
    own, first, second, outs, full = (
        refs[:count],
        refs[count : 2 * count],
        refs[2 * count : 3 * count],
        refs[3 * count : -1],
        refs[-1],
    )
    for i in range(count):
        high, low = halves(own[i][0] + first[i][0] + second[i][...])
        a = jnp.concatenate([high[:K], low[:K]], 0)
        b = jnp.concatenate([high[K:], low[K:]], 0)
        s = lax.dot_general(a, b, ROWS_BY_ROWS, preferred_element_type=jnp.float32)
        full[...] = s[:K, :K] + (s[:K, K:] + s[K:, :K] + s[K:, K:])
        for n, out in enumerate(outs):
            out[i] = full[pl.ds(pl.multiple_of(dest[n] * width, 8), width), :]


def sketches(dest, own, first, second, width):
    count = len(own)
    return pl.pallas_call(
        functools.partial(sketch_kernel, count, width),
        in_specs=[SCALARS] + [WHOLE] * (3 * count),
        out_specs=[WHOLE] * 4,
        out_shape=[pltpu.VMEM((count, width, K), jnp.float32)] * 4,
        scratch_shapes=[pltpu.VMEM((K, K), jnp.float32)],
        cost_estimate=pl.CostEstimate(
            flops=8 * count * LEN * K * K, bytes_accessed=count * 2**19, transcendentals=0
        ),
    )(dest, *own, *first, *second)


def split_kernel(place, mine, other, high, low):
    count, depth = mine.shape
    for n, x in enumerate((mine, other)):
        at = pl.ds(pl.multiple_of((place[0] ^ n) * count, 16), count)
        for lo in range(0, depth, 512):
            h, l = halves(x[:, lo : lo + 512])
            high[at, lo : lo + 512] = h
            low[at, lo : lo + 512] = l


def split(core, mine, other, after=None):
    count, depth = mine.shape
    if after is not None:
        core = lax.optimization_barrier((core, after))[0]
    return pl.pallas_call(
        split_kernel,
        in_specs=[SCALARS, WHOLE, WHOLE],
        out_specs=[WHOLE] * 2,
        out_shape=[pltpu.VMEM((2 * count, depth), jnp.bfloat16)] * 2,
        compiler_params=pltpu.CompilerParams(vmem_limit_bytes=16 * 2**20),
        cost_estimate=pl.CostEstimate(
            flops=8 * count * depth, bytes_accessed=16 * count * depth, transcendentals=0
        ),
    )(core, mine, other)


def score_kernel(pair, place, own, near, skip, across, *refs):
    parts, out, cat = refs[:4], refs[4], refs[5]
    z, chip = place[0], place[1]
    width = own.shape[1]
    count = 4 * pair
    for layer in range(2):
        for r in range(width):
            lanes = slice((layer * width + r) * K, (layer * width + r + 1) * K)
            mine = slice(layer * pair, (layer + 1) * pair)
            cut = [x[mine, r, :] for x in (own, near, skip, across)]
            for b in range(4):
                pick = jnp.where(z == b ^ 2, cut[2], jnp.where(z == 3 - b, cut[3], cut[0]))
                high, low = halves(jnp.where(z == b ^ 1, cut[1], pick))
                cat[b * pair : (b + 1) * pair, lanes] = high.astype(jnp.float32)
                cat[count + b * pair : count + (b + 1) * pair, lanes] = low.astype(jnp.float32)
    s = cat[...].astype(jnp.bfloat16)
    totals = []
    for high, low in (parts[:2], parts[2:]):
        d = lax.dot_general(s, high[...], ROWS_BY_ROWS, preferred_element_type=jnp.float32)
        d += lax.dot_general(s, low[...], ROWS_BY_ROWS, preferred_element_type=jnp.float32)
        totals.append((d[:count] + d[count:]) * (1.0 / (LEN**0.5 * K)))
    mine, other = totals
    out[...] = jnp.concatenate(
        [jnp.where(chip == 0, mine, other), jnp.where(chip == 0, other, mine)], 1
    )


def score(place, cuts, parts, pair):
    queries, depth = parts[0].shape
    return pl.pallas_call(
        functools.partial(score_kernel, pair),
        in_specs=[SCALARS] + [WHOLE] * 8,
        out_specs=WHOLE,
        out_shape=pltpu.VMEM((4 * pair, 2 * queries), jnp.float32),
        scratch_shapes=[pltpu.VMEM((8 * pair, depth), jnp.float32)],
        compiler_params=pltpu.CompilerParams(vmem_limit_bytes=24 * 2**20),
        cost_estimate=pl.CostEstimate(
            flops=64 * queries * depth, bytes_accessed=8 * queries * depth, transcendentals=0
        ),
    )(place, *cuts, *parts)


def line(
    layer_input, up_grad, hidden_input, down_grad, in_up, out_up, in_down, out_down, query_sketch
):
    pair = layer_input.shape[0] // LEN // 4
    width = K // 4
    z = lax.axis_index("tensor").astype(jnp.int32)
    dp = lax.axis_index("dp").astype(jnp.int32)
    layers = (
        (layer_input, up_grad, in_up, out_up),
        (hidden_input, down_grad, in_down, out_down),
    )

    def of(owner, j):
        return owner * pair + j

    def leaving(k):
        return k // pair, [of(z ^ 1, k % pair), of(z ^ 2, k % pair)]

    def staying(k):
        return k // pair, [of(z, k % pair), of(3 - z, k % pair)]

    queries = query_sketch.reshape(query_sketch.shape[0], -1, K)
    by_core = [(0, 1), (1, 0), (2, 3), (3, 2)]
    by_chip = [(0, 2), (2, 0), (1, 3), (3, 1)]
    core = (dp & 1).reshape(1)

    def across(stay, first, after=None):
        if after is not None:
            stay = lax.optimization_barrier((stay, after))[0]
        return stay[1] + first[1]

    chunks = 2 * pair
    stay, first, second = [], [], []
    (out,) = project(layers, [leaving(0)], load=True)
    first.append(send(out, NEAR))
    order = out
    for k in range(chunks):
        if k == 0:
            out, kept, flat = project(layers, [leaving(1), staying(0)], after=order, queries=queries)
            other_core = send(flat, by_core, "dp")
            other_chip = send(flat, by_chip, "dp")
        elif k < chunks - 1:
            out, kept = project(layers, [leaving(k + 1), staying(k)], after=order)
        else:
            (kept,) = project(layers, [staying(k)], after=order)
        stay.append(kept)
        if k < chunks - 1:
            first.append(send(out, NEAR))
            order = (out,) + tuple(second[-1:])
        else:
            own_chip = split(core, flat, other_core, after=kept)
            order = (own_chip[0],) + tuple(second[-1:])
        order = across(kept, first[k], order)
        second.append(send(order, ACROSS))
    other_chip = lax.optimization_barrier((other_chip, order))[0]
    other_both = send(other_chip, by_core, "dp")
    parts = own_chip + split(core, other_chip, other_both)

    dest = jnp.stack([z, z ^ 1, z ^ 2, 3 - z])
    own, near, skip, far = sketches(dest, stay, first, second, width)
    cuts = [own, send(near, NEAR), send(skip, SKIP), send(far, ACROSS)]
    partial = score(jnp.stack([z, dp >> 1]), cuts, parts, pair)
    partial = partial + send(partial, NEAR)
    return partial + send(partial, SKIP)


def own_rows(full, width):
    return lax.dynamic_slice_in_dim(full, lax.axis_index("tensor") * width, width, 1)


def layer_sketch(left, right, examples):
    left3 = left.reshape(examples, LEN, left.shape[1])
    right3 = right.reshape(examples, LEN, right.shape[1])
    return jnp.einsum("elr,elc->erc", left3, right3, precision=lax.Precision.HIGHEST) / jnp.sqrt(
        jnp.float32(LEN)
    )


def wide(
    layer_input, up_grad, hidden_input, down_grad, in_up, out_up, in_down, out_down, query_sketch
):
    width = K // lax.axis_size("tensor")
    examples = layer_input.shape[0] // LEN
    pairs = (
        (layer_input, in_up),
        (up_grad, out_up),
        (hidden_input, in_down),
        (down_grad, out_down),
    )
    a_up, b_up, a_down, b_down = lax.psum(
        tuple(jnp.dot(x, p.T, preferred_element_type=jnp.float32) for x, p in pairs), "tensor"
    )
    sketch = jnp.stack(
        [
            layer_sketch(own_rows(a_up, width), b_up, examples),
            layer_sketch(own_rows(a_down, width), b_down, examples),
        ],
        axis=1,
    )
    partial_total = jnp.einsum(
        "elrc,qlrc->qe",
        sketch,
        lax.all_gather(query_sketch, "dp", axis=0, tiled=True),
        precision=lax.Precision.HIGHEST,
    )
    return lax.psum(partial_total, "tensor").T / jnp.float32(K)


def solution(mesh):
    placed = (
        P(("parts", "dp"), "tensor"),
        P(("parts", "dp"), "tensor"),
        P(("parts", "dp"), "tensor"),
        P(("parts", "dp"), "tensor"),
        P(None, "tensor"),
        P(None, "tensor"),
        P(None, "tensor"),
        P(None, "tensor"),
        P(("parts", "dp"), None, "tensor", None),
    )
    return jax.shard_map(
        line if mesh.shape["tensor"] == 4 and mesh.shape["dp"] == 4 else wide,
        mesh=mesh,
        in_specs=placed,
        out_specs=P(("parts", "dp"), None),
        check_vma=False,
    )
```

```python
import functools

import jax
import jax.numpy as jnp
from jax import lax
from jax.experimental import pallas as pl
from jax.experimental.pallas import tpu as pltpu
from jax.sharding import PartitionSpec as P

K = 128
LEN = 256
PIECE = 1024
AHEAD = 4
ROWS_BY_ROWS = (((1,), (1,)), ((), ()))
NEAR = [(0, 1), (1, 0), (2, 3), (3, 2)]
SKIP = [(0, 2), (2, 0), (1, 3), (3, 1)]
ACROSS = [(0, 3), (3, 0), (1, 2), (2, 1)]

WHOLE = pl.BlockSpec(memory_space=pltpu.VMEM)
SCALARS = pl.BlockSpec(memory_space=pltpu.SMEM)
OUTSIDE = pl.BlockSpec(memory_space=pltpu.HBM)


def here(x):
    return pltpu.with_memory_space_constraint(x, pltpu.VMEM)


def there(x):
    return pltpu.with_memory_space_constraint(x, pltpu.HBM)


def send(x, pairs, axis="tensor"):
    return lax.ppermute(x, axis, pairs)


def halves(x):
    high = x.astype(jnp.bfloat16)
    return high, (x - high.astype(jnp.float32)).astype(jnp.bfloat16)


def pieces(width):
    return [(lo, min(lo + PIECE, width)) for lo in range(0, width, PIECE)]


def project_kernel(jobs, load, index, *refs):
    operands, refs = refs[:8], refs[8:]
    arrays, (slots, sem, *loaded) = refs[: len(jobs)], refs[len(jobs) :]
    depth = slots.shape[0]
    steps = []
    number = 0
    for array, (layer, count) in zip(arrays, jobs):
        left, right, p_left, p_right = operands[4 * layer : 4 * layer + 4]
        for first in range(0, count, 2):
            group = range(first, min(first + 2, count))
            for side, (x, p, row) in enumerate(((left, p_left, 0), (right, p_right, K))):
                for lo, hi in pieces(x.shape[1]):
                    slot = len(steps) % depth
                    copies = [
                        pltpu.make_async_copy(
                            x.at[pl.ds(pl.multiple_of(index[number + i] * LEN, LEN), LEN), lo:hi],
                            slots.at[slot, n * LEN : (n + 1) * LEN, : hi - lo],
                            sem.at[slot, n],
                        )
                        for n, i in enumerate(group)
                    ]
                    if load and first == 0:
                        copies.append(
                            pltpu.make_async_copy(
                                p.at[:, lo:hi], loaded[side].at[:, lo:hi], sem.at[slot, 2]
                            )
                        )
                    outs = [array.at[i] for i in group]
                    steps.append((copies, slot, outs, loaded[side] if load else p, row, lo, hi))
        number += count
    for step in steps[: depth - 1]:
        for copy in step[0]:
            copy.start()
    for n, (copies, slot, outs, p, row, lo, hi) in enumerate(steps):
        for copy in copies:
            copy.wait()
        if n + depth - 1 < len(steps):
            for copy in steps[n + depth - 1][0]:
                copy.start()
        part = lax.dot_general(
            p[:, lo:hi],
            slots[slot, : len(outs) * LEN, : hi - lo],
            ROWS_BY_ROWS,
            preferred_element_type=jnp.float32,
        )
        for m, out in enumerate(outs):
            if lo == 0:
                out[row : row + K, :] = part[:, m * LEN : (m + 1) * LEN]
            else:
                out[row : row + K, :] += part[:, m * LEN : (m + 1) * LEN]


def project(layers, jobs, load=False, after=None):
    index = jnp.stack([i for _, group in jobs for i in group]).astype(jnp.int32)
    if after is not None:
        index = lax.optimization_barrier((index, after))[0]
    jobs = [(layer, len(group)) for layer, group in jobs]
    dtype = layers[0][0].dtype
    scratch = [
        pltpu.VMEM((AHEAD + 1, 2 * LEN, PIECE), dtype),
        pltpu.SemaphoreType.DMA((AHEAD + 1, 3)),
    ]
    if load:
        scratch += [pltpu.VMEM(p.shape, dtype) for p in layers[jobs[0][0]][2:]]
    place = there if load else here
    operands, specs = [], []
    for layer, (left, right, p_left, p_right) in enumerate(layers):
        used = layer in [job[0] for job in jobs]
        operands += [there(left), there(right)]
        operands += [place(p) if used else there(p) for p in (p_left, p_right)]
        specs += [OUTSIDE, OUTSIDE] + [OUTSIDE if load or not used else WHOLE] * 2
    return pl.pallas_call(
        functools.partial(project_kernel, jobs, load),
        in_specs=[SCALARS] + specs,
        out_specs=[WHOLE] * len(jobs),
        out_shape=[pltpu.VMEM((n, 2 * K, LEN), jnp.float32) for _, n in jobs],
        scratch_shapes=scratch,
        compiler_params=pltpu.CompilerParams(vmem_limit_bytes=12 * 2**20),
        cost_estimate=pl.CostEstimate(
            flops=sum(
                2 * n * LEN * K * (layers[layer][0].shape[1] + layers[layer][1].shape[1])
                for layer, n in jobs
            ),
            bytes_accessed=sum(
                2 * n * LEN * (layers[layer][0].shape[1] + layers[layer][1].shape[1])
                for layer, n in jobs
            ),
            transcendentals=0,
        ),
    )(index, *operands)


def sketch_kernel(count, width, before, dest, *refs):
    own, first, second, made, outs, full = (
        refs[:count],
        refs[count : 2 * count],
        refs[2 * count : 3 * count],
        refs[3 * count : -5],
        refs[-5:-1],
        refs[-1],
    )
    for earlier, out in zip(made, outs):
        out[:before] = earlier[...]
    for i in range(count):
        high, low = halves(own[i][0] + first[i][0] + second[i][...])
        a = jnp.concatenate([high[:K], low[:K]], 0)
        b = jnp.concatenate([high[K:], low[K:]], 0)
        s = lax.dot_general(a, b, ROWS_BY_ROWS, preferred_element_type=jnp.float32)
        full[...] = s[:K, :K] + (s[:K, K:] + s[K:, :K] + s[K:, K:])
        for n, out in enumerate(outs):
            out[before + i] = full[pl.ds(pl.multiple_of(dest[n] * width, 8), width), :]


def sketches(dest, own, first, second, width, made=()):
    count = len(own)
    before = made[0].shape[0] if made else 0
    total = before + count
    return pl.pallas_call(
        functools.partial(sketch_kernel, count, width, before),
        in_specs=[SCALARS] + [WHOLE] * (3 * count + len(made)),
        out_specs=[WHOLE] * 4,
        out_shape=[pltpu.VMEM((total, width, K), jnp.float32)] * 4,
        scratch_shapes=[pltpu.VMEM((K, K), jnp.float32)],
        compiler_params=pltpu.CompilerParams(vmem_limit_bytes=8 * 2**20),
        cost_estimate=pl.CostEstimate(
            flops=8 * count * LEN * K * K, bytes_accessed=count * 2**19, transcendentals=0
        ),
    )(dest, *own, *first, *second, *made)


def split_kernel(place, mine, other, high, low, flat, sem):
    count, rows, _ = mine.shape
    moves = [
        [
            pltpu.make_async_copy(x.at[:, r, :], flat.at[n, :, r * K : (r + 1) * K], sem.at[n, r])
            for r in range(rows)
        ]
        for n, x in enumerate((mine, other))
    ]
    for move in moves[0] + moves[1]:
        move.start()
    step = 4
    for n in range(2):
        at = pl.ds(pl.multiple_of((place[0] ^ n) * count, 16), count)
        for r in range(0, rows, step):
            for move in moves[n][r : r + step]:
                move.wait()
            lanes = slice(r * K, (r + step) * K)
            h, l = halves(flat[n, :, lanes])
            high[at, lanes] = h
            low[at, lanes] = l


def split(core, mine, other, after=None):
    count, rows, _ = mine.shape
    if after is not None:
        core = lax.optimization_barrier((core, after))[0]
    return pl.pallas_call(
        split_kernel,
        in_specs=[SCALARS, OUTSIDE, OUTSIDE],
        out_specs=[WHOLE] * 2,
        out_shape=[pltpu.VMEM((2 * count, rows * K), jnp.bfloat16)] * 2,
        scratch_shapes=[
            pltpu.VMEM((2, count, rows * K), jnp.float32),
            pltpu.SemaphoreType.DMA((2, rows)),
        ],
        compiler_params=pltpu.CompilerParams(vmem_limit_bytes=8 * 2**20),
        cost_estimate=pl.CostEstimate(
            flops=8 * count * rows * K, bytes_accessed=16 * count * rows * K, transcendentals=0
        ),
    )(core, there(mine), there(other))


def score_kernel(chunks, pair, chip, dest, *refs):
    cuts, parts, base, out, cat = refs[:4], refs[4:8], refs[8:-2], refs[-2], refs[-1]
    width = cuts[0].shape[1]
    count = 4 * pair
    used = sorted({k // pair for k in chunks})
    depth = width * K
    cat[...] = jnp.zeros_like(cat)
    for i, k in enumerate(chunks):
        layer, j = divmod(k, pair)
        rows = slice(used.index(layer) * width, (used.index(layer) + 1) * width)
        for n, cut in enumerate(cuts):
            high, low = halves(cut[i])
            cat[dest[n] * pair + j, rows, :] = high.astype(jnp.float32)
            cat[count + dest[n] * pair + j, rows, :] = low.astype(jnp.float32)
    s = jnp.concatenate([cat[:, r, :] for r in range(cat.shape[1])], 1).astype(jnp.bfloat16)
    lanes = slice(used[0] * depth, (used[-1] + 1) * depth)
    totals = []
    for high, low in (parts[:2], parts[2:]):
        d = lax.dot_general(s, high[:, lanes], ROWS_BY_ROWS, preferred_element_type=jnp.float32)
        d += lax.dot_general(s, low[:, lanes], ROWS_BY_ROWS, preferred_element_type=jnp.float32)
        totals.append((d[:count] + d[count:]) * (1.0 / (LEN**0.5 * K)))
    mine, other = totals
    first = chip[0] == 0
    total = jnp.concatenate([jnp.where(first, mine, other), jnp.where(first, other, mine)], 1)
    out[...] = total + base[0][...] if base else total


def score(chip, dest, cuts, parts, chunks, pair, base=None):
    queries, _ = parts[0].shape
    rows = len({k // pair for k in chunks}) * cuts[0].shape[1]
    more = [] if base is None else [base]
    return pl.pallas_call(
        functools.partial(score_kernel, chunks, pair),
        in_specs=[SCALARS, SCALARS] + [WHOLE] * (8 + len(more)),
        out_specs=WHOLE,
        out_shape=pltpu.VMEM((4 * pair, 2 * queries), jnp.float32),
        scratch_shapes=[pltpu.VMEM((8 * pair, rows, K), jnp.float32)],
        compiler_params=pltpu.CompilerParams(vmem_limit_bytes=8 * 2**20),
        cost_estimate=pl.CostEstimate(
            flops=64 * queries * rows * K, bytes_accessed=8 * queries * rows * K, transcendentals=0
        ),
    )(chip, dest, *cuts, *parts, *more)


def line(
    layer_input, up_grad, hidden_input, down_grad, in_up, out_up, in_down, out_down, query_sketch
):
    pair = layer_input.shape[0] // LEN // 4
    width = K // 4
    z = lax.axis_index("tensor").astype(jnp.int32)
    dp = lax.axis_index("dp").astype(jnp.int32)
    layers = (
        (layer_input, up_grad, in_up, out_up),
        (hidden_input, down_grad, in_down, out_down),
    )

    def of(owner, j):
        return owner * pair + j

    def leaving(k):
        return k // pair, [of(z ^ 1, k % pair), of(z ^ 2, k % pair)]

    def staying(k):
        return k // pair, [of(z, k % pair), of(3 - z, k % pair)]

    queries = query_sketch.reshape(query_sketch.shape[0], -1, K)
    by_core = [(0, 1), (1, 0), (2, 3), (3, 2)]
    by_chip = [(0, 2), (2, 0), (1, 3), (3, 1)]
    core = (dp & 1).reshape(1)

    def across(stay, first, after=None):
        if after is not None:
            stay = lax.optimization_barrier((stay, after))[0]
        return stay[1] + first[1]

    chunks = 2 * pair
    chip = (dp >> 1).reshape(1)
    dest = jnp.stack([z, z ^ 1, z ^ 2, 3 - z])
    stay, first, second = [], [], []
    (out,) = project(layers, [leaving(0)], load=True)
    first.append(send(out, NEAR))
    order = out
    queries = lax.optimization_barrier((queries, out))[0]
    other_core = send(queries, by_core, "dp")
    other_chip = send(queries, by_chip, "dp")
    for k in range(chunks):
        if k < chunks - 1:
            out, kept = project(layers, [leaving(k + 1), staying(k)], after=order)
            first.append(send(out, NEAR))
            order = (out,)
        else:
            (kept,) = project(layers, [staying(k)], after=order)
            parts = split(core, queries, other_core, after=kept)
            order = (parts[0],)
        stay.append(kept)
        order = across(kept, first[k], order + tuple(second[-1:]))
        second.append(send(order, ACROSS))
    other_chip = lax.optimization_barrier((other_chip, order))[0]
    parts += split(core, other_chip, send(other_chip, by_core, "dp"))
    few = list(range(chunks - 1))
    made = sketches(
        lax.optimization_barrier((dest, order))[0],
        [stay[k] for k in few],
        [first[k] for k in few],
        [second[k] for k in few],
        width,
    )
    own, near, skip, far = sketches(dest, stay[-1:], first[-1:], second[-1:], width, made=made)
    cuts = [own, send(near, NEAR), send(skip, SKIP), send(far, ACROSS)]
    partial = score(chip, dest, cuts, parts, list(range(chunks)), pair)
    partial = partial + send(partial, NEAR)
    return partial + send(partial, SKIP)


def own_rows(full, width):
    return lax.dynamic_slice_in_dim(full, lax.axis_index("tensor") * width, width, 1)


def layer_sketch(left, right, examples):
    left3 = left.reshape(examples, LEN, left.shape[1])
    right3 = right.reshape(examples, LEN, right.shape[1])
    return jnp.einsum("elr,elc->erc", left3, right3, precision=lax.Precision.HIGHEST) / jnp.sqrt(
        jnp.float32(LEN)
    )


def wide(
    layer_input, up_grad, hidden_input, down_grad, in_up, out_up, in_down, out_down, query_sketch
):
    width = K // lax.axis_size("tensor")
    examples = layer_input.shape[0] // LEN
    pairs = (
        (layer_input, in_up),
        (up_grad, out_up),
        (hidden_input, in_down),
        (down_grad, out_down),
    )
    a_up, b_up, a_down, b_down = lax.psum(
        tuple(jnp.dot(x, p.T, preferred_element_type=jnp.float32) for x, p in pairs), "tensor"
    )
    sketch = jnp.stack(
        [
            layer_sketch(own_rows(a_up, width), b_up, examples),
            layer_sketch(own_rows(a_down, width), b_down, examples),
        ],
        axis=1,
    )
    partial_total = jnp.einsum(
        "elrc,qlrc->qe",
        sketch,
        lax.all_gather(query_sketch, "dp", axis=0, tiled=True),
        precision=lax.Precision.HIGHEST,
    )
    return lax.psum(partial_total, "tensor").T / jnp.float32(K)


def solution(mesh):
    placed = (
        P(("parts", "dp"), "tensor"),
        P(("parts", "dp"), "tensor"),
        P(("parts", "dp"), "tensor"),
        P(("parts", "dp"), "tensor"),
        P(None, "tensor"),
        P(None, "tensor"),
        P(None, "tensor"),
        P(None, "tensor"),
        P(("parts", "dp"), None, "tensor", None),
    )
    return jax.shard_map(
        line if mesh.shape["tensor"] == 4 and mesh.shape["dp"] == 4 else wide,
        mesh=mesh,
        in_specs=placed,
        out_specs=P(("parts", "dp"), None),
        check_vma=False,
    )
```

```python
import functools

import jax
import jax.numpy as jnp
from jax import lax
from jax.experimental import pallas as pl
from jax.experimental.pallas import tpu as pltpu
from jax.sharding import PartitionSpec as P

K = 128
LEN = 256
PIECE = 1024
AHEAD = 4
ROWS_BY_ROWS = (((1,), (1,)), ((), ()))
NEAR = [(0, 1), (1, 0), (2, 3), (3, 2)]
SKIP = [(0, 2), (2, 0), (1, 3), (3, 1)]
ACROSS = [(0, 3), (3, 0), (1, 2), (2, 1)]

WHOLE = pl.BlockSpec(memory_space=pltpu.VMEM)
SCALARS = pl.BlockSpec(memory_space=pltpu.SMEM)
OUTSIDE = pl.BlockSpec(memory_space=pltpu.HBM)


def here(x):
    return pltpu.with_memory_space_constraint(x, pltpu.VMEM)


def there(x):
    return pltpu.with_memory_space_constraint(x, pltpu.HBM)


def send(x, pairs, axis="tensor"):
    return lax.ppermute(x, axis, pairs)


def halves(x):
    high = x.astype(jnp.bfloat16)
    return high, (x - high.astype(jnp.float32)).astype(jnp.bfloat16)


def pieces(width):
    return [(lo, min(lo + PIECE, width)) for lo in range(0, width, PIECE)]


def project_kernel(jobs, load, index, *refs):
    operands, refs = refs[:8], refs[8:]
    arrays, (slots, sem, *loaded) = refs[: len(jobs)], refs[len(jobs) :]
    depth = slots.shape[0]
    steps = []
    number = 0
    for array, (layer, count) in zip(arrays, jobs):
        left, right, p_left, p_right = operands[4 * layer : 4 * layer + 4]
        for first in range(0, count, 2):
            group = range(first, min(first + 2, count))
            for side, (x, p, row) in enumerate(((left, p_left, 0), (right, p_right, K))):
                for lo, hi in pieces(x.shape[1]):
                    slot = len(steps) % depth
                    copies = [
                        pltpu.make_async_copy(
                            x.at[pl.ds(pl.multiple_of(index[number + i] * LEN, LEN), LEN), lo:hi],
                            slots.at[slot, n * LEN : (n + 1) * LEN, : hi - lo],
                            sem.at[slot, n],
                        )
                        for n, i in enumerate(group)
                    ]
                    if load and first == 0:
                        copies.append(
                            pltpu.make_async_copy(
                                p.at[:, lo:hi], loaded[side].at[:, lo:hi], sem.at[slot, 2]
                            )
                        )
                    outs = [array.at[i] for i in group]
                    steps.append((copies, slot, outs, loaded[side] if load else p, row, lo, hi))
        number += count
    for step in steps[: depth - 1]:
        for copy in step[0]:
            copy.start()
    for n, (copies, slot, outs, p, row, lo, hi) in enumerate(steps):
        for copy in copies:
            copy.wait()
        if n + depth - 1 < len(steps):
            for copy in steps[n + depth - 1][0]:
                copy.start()
        part = lax.dot_general(
            p[:, lo:hi],
            slots[slot, : len(outs) * LEN, : hi - lo],
            ROWS_BY_ROWS,
            preferred_element_type=jnp.float32,
        )
        for m, out in enumerate(outs):
            if lo == 0:
                out[row : row + K, :] = part[:, m * LEN : (m + 1) * LEN]
            else:
                out[row : row + K, :] += part[:, m * LEN : (m + 1) * LEN]


def project(layers, jobs, load=False, after=None):
    index = jnp.stack([i for _, group in jobs for i in group]).astype(jnp.int32)
    if after is not None:
        index = lax.optimization_barrier((index, after))[0]
    jobs = [(layer, len(group)) for layer, group in jobs]
    dtype = layers[0][0].dtype
    scratch = [
        pltpu.VMEM((AHEAD + 1, 2 * LEN, PIECE), dtype),
        pltpu.SemaphoreType.DMA((AHEAD + 1, 3)),
    ]
    if load:
        scratch += [pltpu.VMEM(p.shape, dtype) for p in layers[jobs[0][0]][2:]]
    place = there if load else here
    operands, specs = [], []
    for layer, (left, right, p_left, p_right) in enumerate(layers):
        used = layer in [job[0] for job in jobs]
        operands += [there(left), there(right)]
        operands += [place(p) if used else there(p) for p in (p_left, p_right)]
        specs += [OUTSIDE, OUTSIDE] + [OUTSIDE if load or not used else WHOLE] * 2
    return pl.pallas_call(
        functools.partial(project_kernel, jobs, load),
        in_specs=[SCALARS] + specs,
        out_specs=[WHOLE] * len(jobs),
        out_shape=[pltpu.VMEM((n, 2 * K, LEN), jnp.float32) for _, n in jobs],
        scratch_shapes=scratch,
        compiler_params=pltpu.CompilerParams(vmem_limit_bytes=12 * 2**20),
        cost_estimate=pl.CostEstimate(
            flops=sum(
                2 * n * LEN * K * (layers[layer][0].shape[1] + layers[layer][1].shape[1])
                for layer, n in jobs
            ),
            bytes_accessed=sum(
                2 * n * LEN * (layers[layer][0].shape[1] + layers[layer][1].shape[1])
                for layer, n in jobs
            ),
            transcendentals=0,
        ),
    )(index, *operands)


def sketch_kernel(count, width, dest, *refs):
    own, first, second, outs, full = (
        refs[:count],
        refs[count : 2 * count],
        refs[2 * count : 3 * count],
        refs[-5:-1],
        refs[-1],
    )
    for i in range(count):
        high, low = halves(own[i][0] + first[i][0] + second[i][...])
        a = jnp.concatenate([high[:K], low[:K]], 0)
        b = jnp.concatenate([high[K:], low[K:]], 0)
        s = lax.dot_general(a, b, ROWS_BY_ROWS, preferred_element_type=jnp.float32)
        full[...] = s[:K, :K] + (s[:K, K:] + s[K:, :K] + s[K:, K:])
        for n, out in enumerate(outs):
            out[i] = full[pl.ds(pl.multiple_of(dest[n] * width, 8), width), :]


def sketches(dest, own, first, second, width):
    count = len(own)
    return pl.pallas_call(
        functools.partial(sketch_kernel, count, width),
        in_specs=[SCALARS] + [WHOLE] * (3 * count),
        out_specs=[WHOLE] * 4,
        out_shape=[pltpu.VMEM((count, width, K), jnp.float32)] * 4,
        scratch_shapes=[pltpu.VMEM((K, K), jnp.float32)],
        compiler_params=pltpu.CompilerParams(vmem_limit_bytes=8 * 2**20),
        cost_estimate=pl.CostEstimate(
            flops=8 * count * LEN * K * K, bytes_accessed=count * 2**19, transcendentals=0
        ),
    )(dest, *own, *first, *second)


def split_kernel(place, mine, other, high, low, flat, sem):
    count, rows, _ = mine.shape
    moves = [
        [
            pltpu.make_async_copy(x.at[:, r, :], flat.at[n, :, r * K : (r + 1) * K], sem.at[n, r])
            for r in range(rows)
        ]
        for n, x in enumerate((mine, other))
    ]
    for move in moves[0] + moves[1]:
        move.start()
    step = 4
    for n in range(2):
        at = pl.ds(pl.multiple_of((place[0] ^ n) * count, 16), count)
        for r in range(0, rows, step):
            for move in moves[n][r : r + step]:
                move.wait()
            lanes = slice(r * K, (r + step) * K)
            h, l = halves(flat[n, :, lanes])
            high[at, lanes] = h
            low[at, lanes] = l


def split(core, mine, other, after=None):
    count, rows, _ = mine.shape
    if after is not None:
        core = lax.optimization_barrier((core, after))[0]
    return pl.pallas_call(
        split_kernel,
        in_specs=[SCALARS, OUTSIDE, OUTSIDE],
        out_specs=[WHOLE] * 2,
        out_shape=[pltpu.VMEM((2 * count, rows * K), jnp.bfloat16)] * 2,
        scratch_shapes=[
            pltpu.VMEM((2, count, rows * K), jnp.float32),
            pltpu.SemaphoreType.DMA((2, rows)),
        ],
        compiler_params=pltpu.CompilerParams(vmem_limit_bytes=8 * 2**20),
        cost_estimate=pl.CostEstimate(
            flops=8 * count * rows * K, bytes_accessed=16 * count * rows * K, transcendentals=0
        ),
    )(core, there(mine), there(other))


def score_kernel(chunks, pair, chip, dest, *refs):
    sets = [refs[4 * n : 4 * n + 4] for n in range(len(chunks))]
    parts, out, cat = refs[-6:-2], refs[-2], refs[-1]
    width = sets[0][0].shape[1]
    count = 4 * pair
    for few, cuts in zip(chunks, sets):
        for i, k in enumerate(few):
            layer, j = divmod(k, pair)
            rows = slice(layer * width, (layer + 1) * width)
            for n, cut in enumerate(cuts):
                high, low = halves(cut[i])
                cat[dest[n] * pair + j, rows, :] = high.astype(jnp.float32)
                cat[count + dest[n] * pair + j, rows, :] = low.astype(jnp.float32)
    s = jnp.concatenate([cat[:, r, :] for r in range(cat.shape[1])], 1).astype(jnp.bfloat16)
    totals = []
    for high, low in (parts[:2], parts[2:]):
        d = lax.dot_general(s, high[...], ROWS_BY_ROWS, preferred_element_type=jnp.float32)
        d += lax.dot_general(s, low[...], ROWS_BY_ROWS, preferred_element_type=jnp.float32)
        totals.append((d[:count] + d[count:]) * (1.0 / (LEN**0.5 * K)))
    mine, other = totals
    first = chip[0] == 0
    total = jnp.concatenate([jnp.where(first, mine, other), jnp.where(first, other, mine)], 1)
    out[...] = total


def score(chip, dest, sets, parts, chunks, pair):
    queries, depth = parts[0].shape
    return pl.pallas_call(
        functools.partial(score_kernel, chunks, pair),
        in_specs=[SCALARS, SCALARS] + [WHOLE] * (4 * len(sets) + 4),
        out_specs=WHOLE,
        out_shape=pltpu.VMEM((4 * pair, 2 * queries), jnp.float32),
        scratch_shapes=[pltpu.VMEM((8 * pair, depth // K, K), jnp.float32)],
        compiler_params=pltpu.CompilerParams(vmem_limit_bytes=8 * 2**20),
        cost_estimate=pl.CostEstimate(
            flops=64 * queries * depth, bytes_accessed=8 * queries * depth, transcendentals=0
        ),
    )(chip, dest, *[cut for cuts in sets for cut in cuts], *parts)


def line(
    layer_input, up_grad, hidden_input, down_grad, in_up, out_up, in_down, out_down, query_sketch
):
    pair = layer_input.shape[0] // LEN // 4
    width = K // 4
    z = lax.axis_index("tensor").astype(jnp.int32)
    dp = lax.axis_index("dp").astype(jnp.int32)
    layers = (
        (layer_input, up_grad, in_up, out_up),
        (hidden_input, down_grad, in_down, out_down),
    )

    def of(owner, j):
        return owner * pair + j

    def leaving(k):
        return k // pair, [of(z ^ 1, k % pair), of(z ^ 2, k % pair)]

    def staying(k):
        return k // pair, [of(z, k % pair), of(3 - z, k % pair)]

    queries = query_sketch.reshape(query_sketch.shape[0], -1, K)
    by_core = [(0, 1), (1, 0), (2, 3), (3, 2)]
    by_chip = [(0, 2), (2, 0), (1, 3), (3, 1)]
    core = (dp & 1).reshape(1)

    def across(stay, first, after=None):
        if after is not None:
            stay = lax.optimization_barrier((stay, after))[0]
        return stay[1] + first[1]

    chunks = 2 * pair
    chip = (dp >> 1).reshape(1)
    dest = jnp.stack([z, z ^ 1, z ^ 2, 3 - z])
    stay, first, second = [], [], []
    (out,) = project(layers, [leaving(0)], load=True)
    first.append(send(out, NEAR))
    order = out
    queries = lax.optimization_barrier((queries, out))[0]
    other_core = send(queries, by_core, "dp")
    other_chip = send(queries, by_chip, "dp")
    for k in range(chunks):
        if k < chunks - 1:
            out, kept = project(layers, [leaving(k + 1), staying(k)], after=order)
            first.append(send(out, NEAR))
            order = (out,)
        else:
            (kept,) = project(layers, [staying(k)], after=order)
            parts = split(core, queries, other_core, after=kept)
            order = (parts[0],)
        stay.append(kept)
        order = across(kept, first[k], order + tuple(second[-1:]))
        second.append(send(order, ACROSS))
    other_chip = lax.optimization_barrier((other_chip, order))[0]
    parts += split(core, other_chip, send(other_chip, by_core, "dp"))
    few, last = list(range(chunks - 1)), [chunks - 1]

    def cuts_of(these, to):
        own, near, skip, far = sketches(
            to, [stay[k] for k in these], [first[k] for k in these], [second[k] for k in these], width
        )
        return [own, send(near, NEAR), send(skip, SKIP), send(far, ACROSS)]

    early = cuts_of(few, lax.optimization_barrier((dest, order))[0])
    late = cuts_of(last, dest)
    partial = score(chip, dest, [early, late], parts, [few, last], pair)
    partial = partial + send(partial, NEAR)
    return partial + send(partial, SKIP)


def own_rows(full, width):
    return lax.dynamic_slice_in_dim(full, lax.axis_index("tensor") * width, width, 1)


def layer_sketch(left, right, examples):
    left3 = left.reshape(examples, LEN, left.shape[1])
    right3 = right.reshape(examples, LEN, right.shape[1])
    return jnp.einsum("elr,elc->erc", left3, right3, precision=lax.Precision.HIGHEST) / jnp.sqrt(
        jnp.float32(LEN)
    )


def wide(
    layer_input, up_grad, hidden_input, down_grad, in_up, out_up, in_down, out_down, query_sketch
):
    width = K // lax.axis_size("tensor")
    examples = layer_input.shape[0] // LEN
    pairs = (
        (layer_input, in_up),
        (up_grad, out_up),
        (hidden_input, in_down),
        (down_grad, out_down),
    )
    a_up, b_up, a_down, b_down = lax.psum(
        tuple(jnp.dot(x, p.T, preferred_element_type=jnp.float32) for x, p in pairs), "tensor"
    )
    sketch = jnp.stack(
        [
            layer_sketch(own_rows(a_up, width), b_up, examples),
            layer_sketch(own_rows(a_down, width), b_down, examples),
        ],
        axis=1,
    )
    partial_total = jnp.einsum(
        "elrc,qlrc->qe",
        sketch,
        lax.all_gather(query_sketch, "dp", axis=0, tiled=True),
        precision=lax.Precision.HIGHEST,
    )
    return lax.psum(partial_total, "tensor").T / jnp.float32(K)


def solution(mesh):
    placed = (
        P(("parts", "dp"), "tensor"),
        P(("parts", "dp"), "tensor"),
        P(("parts", "dp"), "tensor"),
        P(("parts", "dp"), "tensor"),
        P(None, "tensor"),
        P(None, "tensor"),
        P(None, "tensor"),
        P(None, "tensor"),
        P(("parts", "dp"), None, "tensor", None),
    )
    return jax.shard_map(
        line if mesh.shape["tensor"] == 4 and mesh.shape["dp"] == 4 else wide,
        mesh=mesh,
        in_specs=placed,
        out_specs=P(("parts", "dp"), None),
        check_vma=False,
    )
```

```python
import functools

import jax
import jax.numpy as jnp
from jax import lax
from jax.experimental import pallas as pl
from jax.experimental.pallas import tpu as pltpu
from jax.sharding import PartitionSpec as P

K = 128
LEN = 256
PIECE = 1024
AHEAD = 4
ROWS_BY_ROWS = (((1,), (1,)), ((), ()))
NEAR = [(0, 1), (1, 0), (2, 3), (3, 2)]
SKIP = [(0, 2), (2, 0), (1, 3), (3, 1)]
ACROSS = [(0, 3), (3, 0), (1, 2), (2, 1)]

WHOLE = pl.BlockSpec(memory_space=pltpu.VMEM)
SCALARS = pl.BlockSpec(memory_space=pltpu.SMEM)
OUTSIDE = pl.BlockSpec(memory_space=pltpu.HBM)


def here(x):
    return pltpu.with_memory_space_constraint(x, pltpu.VMEM)


def there(x):
    return pltpu.with_memory_space_constraint(x, pltpu.HBM)


def send(x, pairs, axis="tensor"):
    return lax.ppermute(x, axis, pairs)


def halves(x):
    high = x.astype(jnp.bfloat16)
    return high, (x - high.astype(jnp.float32)).astype(jnp.bfloat16)


def pieces(width):
    return [(lo, min(lo + PIECE, width)) for lo in range(0, width, PIECE)]


def project_kernel(jobs, load, index, *refs):
    operands, refs = refs[:8], refs[8:]
    arrays, (slots, sem, *loaded) = refs[: len(jobs)], refs[len(jobs) :]
    depth = slots.shape[0]
    steps = []
    number = 0
    for array, (layer, count) in zip(arrays, jobs):
        left, right, p_left, p_right = operands[4 * layer : 4 * layer + 4]
        for first in range(0, count, 2):
            group = range(first, min(first + 2, count))
            for side, (x, p, row) in enumerate(((left, p_left, 0), (right, p_right, K))):
                for lo, hi in pieces(x.shape[1]):
                    slot = len(steps) % depth
                    copies = [
                        pltpu.make_async_copy(
                            x.at[pl.ds(pl.multiple_of(index[number + i] * LEN, LEN), LEN), lo:hi],
                            slots.at[slot, n * LEN : (n + 1) * LEN, : hi - lo],
                            sem.at[slot, n],
                        )
                        for n, i in enumerate(group)
                    ]
                    if load and first == 0:
                        copies.append(
                            pltpu.make_async_copy(
                                p.at[:, lo:hi], loaded[side].at[:, lo:hi], sem.at[slot, 2]
                            )
                        )
                    outs = [array.at[i] for i in group]
                    steps.append((copies, slot, outs, loaded[side] if load else p, row, lo, hi))
        number += count
    for step in steps[: depth - 1]:
        for copy in step[0]:
            copy.start()
    for n, (copies, slot, outs, p, row, lo, hi) in enumerate(steps):
        for copy in copies:
            copy.wait()
        if n + depth - 1 < len(steps):
            for copy in steps[n + depth - 1][0]:
                copy.start()
        part = lax.dot_general(
            p[:, lo:hi],
            slots[slot, : len(outs) * LEN, : hi - lo],
            ROWS_BY_ROWS,
            preferred_element_type=jnp.float32,
        )
        for m, out in enumerate(outs):
            if lo == 0:
                out[row : row + K, :] = part[:, m * LEN : (m + 1) * LEN]
            else:
                out[row : row + K, :] += part[:, m * LEN : (m + 1) * LEN]


def project(layers, jobs, load=False, after=None):
    index = jnp.stack([i for _, group in jobs for i in group]).astype(jnp.int32)
    if after is not None:
        index = lax.optimization_barrier((index, after))[0]
    jobs = [(layer, len(group)) for layer, group in jobs]
    dtype = layers[0][0].dtype
    scratch = [
        pltpu.VMEM((AHEAD + 1, 2 * LEN, PIECE), dtype),
        pltpu.SemaphoreType.DMA((AHEAD + 1, 3)),
    ]
    if load:
        scratch += [pltpu.VMEM(p.shape, dtype) for p in layers[jobs[0][0]][2:]]
    place = there if load else here
    operands, specs = [], []
    for layer, (left, right, p_left, p_right) in enumerate(layers):
        used = layer in [job[0] for job in jobs]
        operands += [there(left), there(right)]
        operands += [place(p) if used else there(p) for p in (p_left, p_right)]
        specs += [OUTSIDE, OUTSIDE] + [OUTSIDE if load or not used else WHOLE] * 2
    return pl.pallas_call(
        functools.partial(project_kernel, jobs, load),
        in_specs=[SCALARS] + specs,
        out_specs=[WHOLE] * len(jobs),
        out_shape=[pltpu.VMEM((n, 2 * K, LEN), jnp.float32) for _, n in jobs],
        scratch_shapes=scratch,
        compiler_params=pltpu.CompilerParams(vmem_limit_bytes=12 * 2**20),
        cost_estimate=pl.CostEstimate(
            flops=sum(
                2 * n * LEN * K * (layers[layer][0].shape[1] + layers[layer][1].shape[1])
                for layer, n in jobs
            ),
            bytes_accessed=sum(
                2 * n * LEN * (layers[layer][0].shape[1] + layers[layer][1].shape[1])
                for layer, n in jobs
            ),
            transcendentals=0,
        ),
    )(index, *operands)


def sketch_kernel(count, width, dest, *refs):
    own, first, second, outs, full = (
        refs[:count],
        refs[count : 2 * count],
        refs[2 * count : 3 * count],
        refs[-5:-1],
        refs[-1],
    )
    for i in range(count):
        high, low = halves(own[i][0] + first[i][0] + second[i][...])
        a = jnp.concatenate([high[:K], low[:K]], 0)
        b = jnp.concatenate([high[K:], low[K:]], 0)
        s = lax.dot_general(a, b, ROWS_BY_ROWS, preferred_element_type=jnp.float32)
        full[...] = s[:K, :K] + (s[:K, K:] + s[K:, :K] + s[K:, K:])
        for n, out in enumerate(outs):
            out[i] = full[pl.ds(pl.multiple_of(dest[n] * width, 8), width), :]


def sketches(dest, own, first, second, width):
    count = len(own)
    return pl.pallas_call(
        functools.partial(sketch_kernel, count, width),
        in_specs=[SCALARS] + [WHOLE] * (3 * count),
        out_specs=[WHOLE] * 4,
        out_shape=[pltpu.VMEM((count, width, K), jnp.float32)] * 4,
        scratch_shapes=[pltpu.VMEM((K, K), jnp.float32)],
        compiler_params=pltpu.CompilerParams(vmem_limit_bytes=8 * 2**20),
        cost_estimate=pl.CostEstimate(
            flops=8 * count * LEN * K * K, bytes_accessed=count * 2**19, transcendentals=0
        ),
    )(dest, *own, *first, *second)


def split_kernel(core, *refs):
    *blocks, high, low, flat, sem = refs
    count, rows, _ = blocks[0].shape
    moves = [
        [
            pltpu.make_async_copy(x.at[:, r, :], flat.at[n, :, r * K : (r + 1) * K], sem.at[n, r])
            for r in range(rows)
        ]
        for n, x in enumerate(blocks)
    ]
    for move in sum(moves, []):
        move.start()
    step = 4
    for n in range(len(blocks)):
        first = (core[0] ^ n) * count if len(blocks) > 1 else 0
        at = pl.ds(pl.multiple_of(first, 16), count)
        for r in range(0, rows, step):
            for move in moves[n][r : r + step]:
                move.wait()
            lanes = slice(r * K, (r + step) * K)
            h, l = halves(flat[n, :, lanes])
            high[at, lanes] = h
            low[at, lanes] = l


def split(core, blocks, after=None):
    number = len(blocks)
    count, rows, _ = blocks[0].shape
    if after is not None:
        core = lax.optimization_barrier((core, after))[0]
    return pl.pallas_call(
        split_kernel,
        in_specs=[SCALARS] + [OUTSIDE] * number,
        out_specs=[WHOLE] * 2,
        out_shape=[pltpu.VMEM((number * count, rows * K), jnp.bfloat16)] * 2,
        scratch_shapes=[
            pltpu.VMEM((number, count, rows * K), jnp.float32),
            pltpu.SemaphoreType.DMA((number, rows)),
        ],
        compiler_params=pltpu.CompilerParams(vmem_limit_bytes=8 * 2**20),
        cost_estimate=pl.CostEstimate(
            flops=4 * number * count * rows * K,
            bytes_accessed=8 * number * count * rows * K,
            transcendentals=0,
        ),
    )(core, *[there(x) for x in blocks])


def score_kernel(chunks, pair, dp, dest, *refs):
    sets = [refs[4 * n : 4 * n + 4] for n in range(len(chunks))]
    parts, out, cat = refs[-8:-2], refs[-2], refs[-1]
    width = sets[0][0].shape[1]
    count = 4 * pair
    for few, cuts in zip(chunks, sets):
        for i, k in enumerate(few):
            layer, j = divmod(k, pair)
            rows = slice(layer * width, (layer + 1) * width)
            for n, cut in enumerate(cuts):
                high, low = halves(cut[i])
                cat[dest[n] * pair + j, rows, :] = high.astype(jnp.float32)
                cat[count + dest[n] * pair + j, rows, :] = low.astype(jnp.float32)
    s = jnp.concatenate([cat[:, r, :] for r in range(cat.shape[1])], 1).astype(jnp.bfloat16)
    totals = []
    for high, low in (parts[:2], parts[2:4], parts[4:]):
        d = lax.dot_general(s, high[...], ROWS_BY_ROWS, preferred_element_type=jnp.float32)
        d += lax.dot_general(s, low[...], ROWS_BY_ROWS, preferred_element_type=jnp.float32)
        totals.append((d[:count] + d[count:]) * (1.0 / (LEN**0.5 * K)))
    mine, same, mate = totals
    second = dp[0] % 2 == 1
    other = jnp.concatenate([jnp.where(second, mate, same), jnp.where(second, same, mate)], 1)
    first = dp[0] < 2
    total = jnp.concatenate([jnp.where(first, mine, other), jnp.where(first, other, mine)], 1)
    out[...] = total


def score(dp, dest, sets, parts, chunks, pair):
    queries, depth = parts[0].shape
    return pl.pallas_call(
        functools.partial(score_kernel, chunks, pair),
        in_specs=[SCALARS, SCALARS] + [WHOLE] * (4 * len(sets) + 6),
        out_specs=WHOLE,
        out_shape=pltpu.VMEM((4 * pair, 2 * queries), jnp.float32),
        scratch_shapes=[pltpu.VMEM((8 * pair, depth // K, K), jnp.float32)],
        compiler_params=pltpu.CompilerParams(vmem_limit_bytes=8 * 2**20),
        cost_estimate=pl.CostEstimate(
            flops=64 * queries * depth, bytes_accessed=8 * queries * depth, transcendentals=0
        ),
    )(dp, dest, *[cut for cuts in sets for cut in cuts], *parts)


def line(
    layer_input, up_grad, hidden_input, down_grad, in_up, out_up, in_down, out_down, query_sketch
):
    pair = layer_input.shape[0] // LEN // 4
    width = K // 4
    z = lax.axis_index("tensor").astype(jnp.int32)
    dp = lax.axis_index("dp").astype(jnp.int32)
    layers = (
        (layer_input, up_grad, in_up, out_up),
        (hidden_input, down_grad, in_down, out_down),
    )

    def of(owner, j):
        return owner * pair + j

    def leaving(k):
        return k // pair, [of(z ^ 1, k % pair), of(z ^ 2, k % pair)]

    def staying(k):
        return k // pair, [of(z, k % pair), of(3 - z, k % pair)]

    queries = query_sketch.reshape(query_sketch.shape[0], -1, K)
    by_core = [(0, 1), (1, 0), (2, 3), (3, 2)]
    by_chip = [(0, 2), (2, 0), (1, 3), (3, 1)]
    core = (dp & 1).reshape(1)

    def across(stay, first, after=None):
        if after is not None:
            stay = lax.optimization_barrier((stay, after))[0]
        return stay[1] + first[1]

    chunks = 2 * pair
    dest = jnp.stack([z, z ^ 1, z ^ 2, 3 - z])
    stay, first, second = [], [], []
    (out,) = project(layers, [leaving(0)], load=True)
    first.append(send(out, NEAR))
    order = out
    queries = lax.optimization_barrier((queries, out))[0]
    other_core = send(queries, by_core, "dp")
    other_chip = send(queries, by_chip, "dp")
    for k in range(chunks):
        if k < chunks - 1:
            out, kept = project(layers, [leaving(k + 1), staying(k)], after=order)
            first.append(send(out, NEAR))
            order = (out,)
        else:
            (kept,) = project(layers, [staying(k)], after=order)
            parts = split(core, [queries, other_core], after=kept)
            order = (parts[0],)
        stay.append(kept)
        order = across(kept, first[k], order + tuple(second[-1:]))
        second.append(send(order, ACROSS))
    other_chip = lax.optimization_barrier((other_chip, order))[0]
    other_both = send(other_chip, by_core, "dp")
    few, last = list(range(chunks - 1)), [chunks - 1]

    def cuts_of(these, to):
        own, near, skip, far = sketches(
            to, [stay[k] for k in these], [first[k] for k in these], [second[k] for k in these], width
        )
        return [own, send(near, NEAR), send(skip, SKIP), send(far, ACROSS)]

    early = cuts_of(few, lax.optimization_barrier((dest, order))[0])
    parts += split(core, [other_chip], after=early[0])
    late = cuts_of(last, lax.optimization_barrier((dest, parts[2]))[0])
    parts += split(core, [other_both])
    partial = score(dp.reshape(1), dest, [early, late], parts, [few, last], pair)
    partial = partial + send(partial, NEAR)
    return partial + send(partial, SKIP)


def own_rows(full, width):
    return lax.dynamic_slice_in_dim(full, lax.axis_index("tensor") * width, width, 1)


def layer_sketch(left, right, examples):
    left3 = left.reshape(examples, LEN, left.shape[1])
    right3 = right.reshape(examples, LEN, right.shape[1])
    return jnp.einsum("elr,elc->erc", left3, right3, precision=lax.Precision.HIGHEST) / jnp.sqrt(
        jnp.float32(LEN)
    )


def wide(
    layer_input, up_grad, hidden_input, down_grad, in_up, out_up, in_down, out_down, query_sketch
):
    width = K // lax.axis_size("tensor")
    examples = layer_input.shape[0] // LEN
    pairs = (
        (layer_input, in_up),
        (up_grad, out_up),
        (hidden_input, in_down),
        (down_grad, out_down),
    )
    a_up, b_up, a_down, b_down = lax.psum(
        tuple(jnp.dot(x, p.T, preferred_element_type=jnp.float32) for x, p in pairs), "tensor"
    )
    sketch = jnp.stack(
        [
            layer_sketch(own_rows(a_up, width), b_up, examples),
            layer_sketch(own_rows(a_down, width), b_down, examples),
        ],
        axis=1,
    )
    partial_total = jnp.einsum(
        "elrc,qlrc->qe",
        sketch,
        lax.all_gather(query_sketch, "dp", axis=0, tiled=True),
        precision=lax.Precision.HIGHEST,
    )
    return lax.psum(partial_total, "tensor").T / jnp.float32(K)


def solution(mesh):
    placed = (
        P(("parts", "dp"), "tensor"),
        P(("parts", "dp"), "tensor"),
        P(("parts", "dp"), "tensor"),
        P(("parts", "dp"), "tensor"),
        P(None, "tensor"),
        P(None, "tensor"),
        P(None, "tensor"),
        P(None, "tensor"),
        P(("parts", "dp"), None, "tensor", None),
    )
    return jax.shard_map(
        line if mesh.shape["tensor"] == 4 and mesh.shape["dp"] == 4 else wide,
        mesh=mesh,
        in_specs=placed,
        out_specs=P(("parts", "dp"), None),
        check_vma=False,
    )
```
